32 devices in a mesh: groups: 2 (over y), gx: 8 (over z, x), gy: 2 (over core).
Axes of the slice: x: 2, y: 2, z: 4, core: 2. Of those that a mesh axis runs over, the one named last changes fastest.
Arguments:
- activations: bfloat16 [128, 16384], P(('groups', 'gy'), 'gx'), parts along dimension 0, may hold values from -6 to 6
- qkv_weight: bfloat16 [16384, 18432], P('gx', 'gy'), may hold values from -0.046875 to 0.046875
- out_weight: bfloat16 [16384, 16384], P('gy', 'gx'), may hold values from -0.046875 to 0.046875
- key_cache: bfloat16 [128, 256, 8, 128], P(('groups', 'gx'), None, 'gy'), parts along dimension 0, may hold values from -600 to 600
- value_cache: bfloat16 [128, 256, 8, 128], P(('groups', 'gx'), None, 'gy'), parts along dimension 0, may hold values from -6 to 6
- lengths: int32 [128], P(('groups', 'gx')), parts along dimension 0, may hold values from 1 to 256, as said below
Outputs:
- attn_out: bfloat16 [128, 16384], P(('groups', 'gy'), 'gx'), parts along dimension 0
The draws below stay inside these ranges and needn't reach their ends.
There are 2 independent parts, one for each index of `groups`. The reference program is written for one: setup_inputs(seed, part) draws one part's arguments, and reference() takes and returns one part's arrays. A program takes and returns all parts, laid end to end along the dimension named above; an argument that names none is the same for every part. Nothing has to cross between parts.
Inputs may be any that keep to these rules, and one draw needn't show every extreme that they name: `lengths`: each request's cached tokens; in every block of 8 requests held by one index of gx some request has all 256 slots filled.
All inputs are finite; a program needn't handle non-finite values.
Results may differ from the reference program's by a relative error of at most 0.015.
Values may be sent and summed in bfloat16 or wider, within the bound.
A program may use at most 128 MiB of HBM per device.

```python
import jax
import jax.numpy as jnp
from jax import lax

D = 16384
HQ = 128
KVH = 8
HD = 128
ROWS_DEV = 8
CTX = 256
GQ = 16
ROWS = 64


def draw_key_cache(key, part):
    key = jax.random.fold_in(key, 11)
    base_key = jax.random.fold_in(key, 0)
    vectors = jnp.clip(jax.random.normal(base_key, (ROWS, CTX, KVH, HD), jnp.float32), -6.0, 6.0)
    return vectors.astype(jnp.bfloat16)


def draw_lengths(key, part):
    key = jax.random.fold_in(key, 7)
    base_key, pick_key = jax.random.split(key)
    base = jax.random.randint(base_key, (ROWS // ROWS_DEV, ROWS_DEV), 1, CTX + 1)
    picked = jax.random.randint(pick_key, (ROWS // ROWS_DEV, 1), 0, ROWS_DEV)
    filled = jnp.arange(ROWS_DEV)[None, :] == picked
    return jnp.where(filled, CTX, base).reshape(ROWS).astype(jnp.int32)


def spiked(entries, own_key, source, target, shards_of, factor):
    def block_of(axis_at):
        return (jnp.arange(entries.shape[axis_at]) // (entries.shape[axis_at] // shards_of)).reshape((-1,) + (1,) * (entries.ndim - 1 - axis_at))

    one_side = jax.random.permutation(own_key, shards_of)[block_of(target)]
    far = (block_of(target) + shards_of // 2) % shards_of
    return jnp.where((block_of(source) == one_side) | (block_of(source) == far), factor * entries, entries)


def level_of(key, dims, cuts, smallest, top_value):
    factor_of, own = 1.0, jax.random.fold_in(key, 6)
    for axis_at, blocks in cuts:
        draws = jnp.exp(jax.random.uniform(jax.random.fold_in(own, axis_at), (blocks,), jnp.float32, smallest / len(cuts), top_value / len(cuts)))
        factor_of = factor_of * jnp.repeat(draws, dims[axis_at] // blocks).reshape([-1 if axis == axis_at else 1 for axis in range(len(dims))])
    return factor_of


def bell_draw(key, extent, scale, most, cuts=(), dtype=jnp.bfloat16):
    gain = level_of(key, extent, cuts, -0.22, 0.18) if cuts else 1.0
    entries = jax.random.normal(key, extent, jnp.float32) * scale * gain
    return jnp.minimum(jnp.maximum(entries, -most), most).astype(dtype)


def gaussian_with(stream_key, shape, scale, limit, cuts, heavy, held_as=jnp.bfloat16):
    array = scale * jax.random.normal(stream_key, shape, jnp.float32)
    if cuts:
        array = array * level_of(stream_key, shape, cuts, -0.22, 0.18)
    return jnp.clip(spiked(array, jax.random.fold_in(stream_key, 3), *heavy), -limit, limit).astype(held_as)


def setup_inputs(seed: int = 0, part: int = 0) -> dict:
    streams_of = jax.random.split(jax.random.key(seed), 7)
    part_splits = jax.random.split(jax.random.fold_in(streams_of[6], part), 7)
    activations = gaussian_with(part_splits[0], (ROWS, D), 1.0, 6.0, ((0, 2), (1, 8)), (1, 0, 8, 2.0))
    qkv_weight = bell_draw(streams_of[1], (D, KVH * (GQ + 2) * HD), D ** -0.5, 0.046875, ((0, 8), (1, 2)))
    out_weight = bell_draw(streams_of[2], (HQ * HD, D), (HQ * HD) ** -0.5, 0.046875, ((0, 2), (1, 8)))
    key_cache = draw_key_cache(jax.random.fold_in(jax.random.fold_in(streams_of[6], part), 71), part)
    value_cache = bell_draw(part_splits[4], (ROWS, CTX, KVH, HD), 1.0, 6.0, ((0, 8), (2, 2)))
    lengths = draw_lengths(jax.random.fold_in(jax.random.fold_in(streams_of[6], part), 71), part)
    return {"activations": activations, "qkv_weight": qkv_weight, "out_weight": out_weight, "key_cache": key_cache, "value_cache": value_cache, "lengths": lengths}


def rotate(vectors, positions):
    half_dim = vectors.shape[-1] // 2
    frequency = 500000.0 ** (-(jnp.arange(half_dim).astype(jnp.float32) * 2.0 / vectors.shape[-1]))
    angles = positions.astype(jnp.float32)[..., None] * frequency
    cosine = jnp.cos(angles)
    sine_part = jnp.sin(angles)
    lower_half = vectors[..., :half_dim]
    upper_half = vectors[..., half_dim:]
    return jnp.concatenate([lower_half * cosine - upper_half * sine_part, upper_half * cosine + lower_half * sine_part], axis=-1)


def attend(queries, new_key, new_value, keys, values, lengths):
    queries = rotate(queries.astype(jnp.float32), lengths[:, None, None]).astype(jnp.bfloat16)
    new_key = rotate(new_key.astype(jnp.float32), lengths[:, None]).astype(jnp.bfloat16)
    scaling = queries.shape[-1] ** -0.5
    scores = jnp.einsum("rgqd,rpgd->rgqp", queries.astype(jnp.float32), keys.astype(jnp.float32)) * scaling
    own_score = jnp.einsum("rgqd,rgd->rgq", queries.astype(jnp.float32), new_key.astype(jnp.float32)) * scaling
    visible = (jnp.arange(keys.shape[1])[None, :] < lengths[:, None])[:, None, None, :]
    masked = jnp.where(visible, scores, -1e30)
    highest = jnp.maximum(jnp.max(masked, axis=-1), own_score)
    raised = jnp.where(visible, jnp.exp(masked - highest[..., None]), 0.0)
    own_raised = jnp.exp(own_score - highest)
    denominator = jnp.sum(raised, axis=-1) + own_raised
    weights = (raised / denominator[..., None]).astype(jnp.bfloat16)
    own_weight = (own_raised / denominator).astype(jnp.bfloat16)
    blended = jnp.einsum("rgqp,rpgd->rgqd", weights.astype(jnp.float32), values.astype(jnp.float32))
    blended = blended + own_weight.astype(jnp.float32)[..., None] * new_value.astype(jnp.float32)[:, :, None, :]
    return blended.astype(jnp.bfloat16)


def reference(activations, qkv_weight, out_weight, key_cache, value_cache, lengths):
    projected = jnp.dot(activations, qkv_weight, preferred_element_type=jnp.float32).astype(jnp.bfloat16)
    projected = projected.reshape(ROWS, KVH, GQ + 2, HD)

    def one_head(kv_group):
        block = lax.dynamic_slice_in_dim(projected, kv_group, 1, 1)
        keys = lax.dynamic_slice_in_dim(key_cache, kv_group, 1, 2)
        values = lax.dynamic_slice_in_dim(value_cache, kv_group, 1, 2)
        return attend(block[:, :, :GQ], block[:, :, GQ], block[:, :, GQ + 1], keys, values, lengths)

    stacked = lax.map(one_head, jnp.arange(KVH).astype(jnp.int32))
    attended = jnp.moveaxis(stacked[:, :, 0], 0, 1).reshape(ROWS, HQ * HD)
    return jnp.dot(attended, out_weight, preferred_element_type=jnp.float32).astype(jnp.bfloat16)
```

```python
import functools

import jax
import jax.numpy as jnp
from jax import lax
from jax.experimental import pallas as pl
from jax.experimental.pallas import tpu as pltpu
from jax.sharding import PartitionSpec as P

MESH = pl.DeviceIdType.MESH
XN, ZN = 2, 4
TILE = 256
SLOTS = 4


def fused_kernel(
    dims, act_hbm, wq_hbm, wo_hbm, key_hbm, val_hbm, cos_ref, sin_ref, len_ref, out_ref,
    act, wbuf, wo, keys, vals, xsend, xkeep, xrecv, zbuf, zrecv, proj, qrows, score, orows,
    att, lhs, acc, psend, precv,
    act_sem, w_sem, wo_sem, kv_sem, xs_sem, xr_sem, zs_sem, zr_sem,
    azs_sem, azr_sem, axs_sem, axr_sem, ps_sem, pr_sem,
):
    groups, gq, hd, piece, pieces, rows_dev = dims
    rows = act.shape[0]
    half_rows = rows // 2
    gx = lax.axis_index("gx")
    gy = lax.axis_index("gy")
    x = lax.rem(gx, XN)
    z = lax.div(gx, XN)
    xpeer = z * XN + (1 - x)
    ypeer = 1 - gy

    def zpeer(d):
        return lax.rem(z + d, ZN) * XN + x

    def zfrom(d):
        return lax.rem(z + ZN - d, ZN) * XN + x

    def w_copy(i):
        cols = pl.ds(pl.multiple_of(i * piece, piece), piece)
        slot = lax.rem(i, SLOTS)
        return pltpu.make_async_copy(wq_hbm.at[:, cols], wbuf.at[slot], w_sem.at[slot])

    group_width = gq * hd

    def wo_copy(j):
        part = pl.ds(pl.multiple_of(j * group_width, group_width), group_width)
        return pltpu.make_async_copy(wo_hbm.at[part], wo.at[part], wo_sem.at[j])

    key_copy = pltpu.make_async_copy(key_hbm, keys, kv_sem.at[0])
    val_copy = pltpu.make_async_copy(val_hbm, vals, kv_sem.at[1])

    def x_copy(i):
        return pltpu.make_async_remote_copy(
            xsend.at[i], xrecv.at[i], xs_sem.at[i], xr_sem.at[i],
            device_id={"gx": xpeer}, device_id_type=MESH)

    def z_copy(i, d):
        return pltpu.make_async_remote_copy(
            zbuf.at[i, lax.rem(z + d, ZN)], zrecv.at[i, d - 1], zs_sem.at[i, d - 1],
            zr_sem.at[i, d - 1], device_id={"gx": zpeer(d)}, device_id_type=MESH)

    def az_copy(j, d):
        return pltpu.make_async_remote_copy(
            att.at[j, gx], att.at[j, gx], azs_sem.at[j, d - 1], azr_sem.at[j, d - 1],
            device_id={"gx": zpeer(d)}, device_id_type=MESH)

    def az_arrival(j, d):
        return pltpu.make_async_remote_copy(
            att.at[j, zfrom(d)], att.at[j, zfrom(d)], azs_sem.at[j, d - 1], azr_sem.at[j, d - 1],
            device_id={"gx": zpeer(d)}, device_id_type=MESH)

    def ax_copy(j, d):
        return pltpu.make_async_remote_copy(
            att.at[j, zfrom(d)], att.at[j, zfrom(d)], axs_sem.at[j, d], axr_sem.at[j, d],
            device_id={"gx": xpeer}, device_id_type=MESH)

    def ax_arrival(j, d):
        block = lax.rem(z + ZN - d, ZN) * XN + (1 - x)
        return pltpu.make_async_remote_copy(
            att.at[j, block], att.at[j, block], axs_sem.at[j, d], axr_sem.at[j, d],
            device_id={"gx": xpeer}, device_id_type=MESH)

    for i in range(SLOTS):
        w_copy(i).start()
    mine = pl.ds(pl.multiple_of(gy * half_rows, half_rows), half_rows)
    theirs = pl.ds(pl.multiple_of(ypeer * half_rows, half_rows), half_rows)
    own_act = pltpu.make_async_copy(act_hbm, act.at[mine], act_sem.at[0])
    own_act.start()

    barrier = pltpu.get_barrier_semaphore()
    for d in range(1, ZN):
        pl.semaphore_signal(barrier, inc=1, device_id={"gx": zpeer(d)}, device_id_type=MESH)
    pl.semaphore_signal(barrier, inc=1, device_id={"gx": xpeer}, device_id_type=MESH)
    pl.semaphore_signal(barrier, inc=1, device_id={"gy": ypeer}, device_id_type=MESH)
    pl.semaphore_wait(barrier, ZN + 1)

    peer_act = pltpu.make_async_remote_copy(
        act_hbm, act.at[mine], act_sem.at[1], act_sem.at[2],
        device_id={"gy": ypeer}, device_id_type=MESH)
    peer_act.start()
    key_copy.start()
    val_copy.start()
    acc[...] = jnp.zeros_like(acc)
    own_act.wait()
    peer_act.wait()

    def project(j):
        def one(p, _):
            i = j * pieces + p
            slot = lax.rem(i, SLOTS)
            w_copy(i).wait()
            for t in range(piece // TILE):
                cols = pl.ds(t * TILE, TILE)
                part = jnp.dot(act[...], wbuf[slot, :, cols], preferred_element_type=jnp.float32)
                part = part.reshape(ZN, XN, rows_dev, TILE)
                first, second = part[:, 0], part[:, 1]
                xkeep[i, :, :, cols] = jnp.where(x == 0, first, second)
                xsend[i, :, :, cols] = jnp.where(x == 0, second, first)
            x_copy(i).start()

            @pl.when(i + SLOTS < groups * pieces)
            def _():
                w_copy(i + SLOTS).start()
            return 0
        lax.fori_loop(0, pieces, one, 0)
        wo_copy(j).start()

    def across_x(j):
        def one(p, _):
            i = j * pieces + p
            x_copy(i).wait_recv()
            zbuf[i] = xkeep[i] + xrecv[i]
            for d in range(1, ZN):
                z_copy(i, d).start()
            return 0
        lax.fori_loop(0, pieces, one, 0)

    def attention(j):
        for p in range(pieces):
            i = j * pieces + p
            for d in range(1, ZN):
                z_copy(i, d).wait_recv()
            total = zbuf[i, z] + zrecv[i, 0] + zrecv[i, 1] + zrecv[i, 2]
            proj[:, p * piece:(p + 1) * piece] = total.astype(jnp.bfloat16).astype(jnp.float32)

        def turned(h):
            v = proj[:, h * hd:(h + 1) * hd]
            swapped = jnp.concatenate([v[:, hd // 2:], v[:, :hd // 2]], axis=1)
            r = v * cos_ref[...] + swapped * sin_ref[...]
            return r.astype(jnp.bfloat16).astype(jnp.float32)

        for h in range(gq):
            qrows[h * rows_dev:(h + 1) * rows_dev, :] = turned(h)
        new_key = turned(gq)
        new_value = proj[:, (gq + 1) * hd:(gq + 2) * hd]
        scaling = hd ** -0.5
        own = []
        for r in range(rows_dev):
            q = qrows[pl.ds(r, gq, stride=rows_dev), :]
            score[r * gq:(r + 1) * gq, :] = lax.dot_general(
                q.astype(jnp.bfloat16), keys[r], (((1,), (1,)), ((), ())),
                preferred_element_type=jnp.float32) * scaling
            own.append(jnp.sum(q * new_key[r:r + 1, :], axis=1, keepdims=True) * scaling)
        own = jnp.concatenate(own, axis=0)
        column = lax.broadcasted_iota(jnp.int32, score.shape, 1)
        seen = (column < len_ref[:, :1]) & (lax.rem(column, groups) == j)
        masked = jnp.where(seen, score[...], -1e30)
        highest = jnp.maximum(jnp.max(masked, axis=1, keepdims=True), own)
        raised = jnp.where(seen, jnp.exp(masked - highest), 0.0)
        own_raised = jnp.exp(own - highest)
        denominator = jnp.sum(raised, axis=1, keepdims=True) + own_raised
        weights = (raised / denominator).astype(jnp.bfloat16)
        own_weight = (own_raised / denominator).astype(jnp.bfloat16).astype(jnp.float32)
        for r in range(rows_dev):
            part = slice(r * gq, (r + 1) * gq)
            blended = jnp.dot(weights[part], vals[r], preferred_element_type=jnp.float32)
            orows[pl.ds(r, gq, stride=rows_dev), :] = blended + own_weight[part] * new_value[r:r + 1, :]
        att[j, gx] = orows[...].astype(jnp.bfloat16)
        for d in range(1, ZN):
            az_copy(j, d).start()
        ax_copy(j, 0).start()

    def relay(j):
        for d in range(1, ZN):
            az_arrival(j, d).wait_recv()
            ax_copy(j, d).start()

    def output(j):
        for d in range(ZN):
            ax_arrival(j, d).wait_recv()
        for b in range(XN * ZN // 2):
            pair = []
            for s in range(2):
                block = att[j, 2 * b + s].astype(jnp.float32)
                pair.append(jnp.concatenate(
                    [block[h * rows_dev:(h + 1) * rows_dev] for h in range(gq)], axis=1))
            lhs[2 * b * rows_dev:2 * (b + 1) * rows_dev, :] = jnp.concatenate(
                pair, axis=0).astype(jnp.bfloat16)
        wo_copy(j).wait()
        depth = pl.ds(pl.multiple_of(j * group_width, group_width), group_width)

        def one(n, _):
            cols = pl.ds(pl.multiple_of(n * TILE, TILE), TILE)
            acc[:, cols] += jnp.dot(lhs[...], wo[depth, cols], preferred_element_type=jnp.float32)
            return 0
        lax.fori_loop(0, acc.shape[1] // TILE, one, 0)

    def step(t, _):
        for delay, stage in enumerate((project, across_x, attention, relay, output)):
            if delay == 2:
                @pl.when(t == 2)
                def _():
                    key_copy.wait()
                    val_copy.wait()

            @pl.when((t >= delay) & (t < groups + delay))
            def _(stage=stage, delay=delay):
                stage(t - delay)
        return 0
    lax.fori_loop(0, groups + 4, step, 0)

    psend[...] = acc[theirs, :].astype(jnp.bfloat16)
    last = pltpu.make_async_remote_copy(
        psend, precv, ps_sem, pr_sem, device_id={"gy": ypeer}, device_id_type=MESH)
    last.start()
    last.wait_recv()
    out_ref[...] = (acc[mine, :] + precv[...].astype(jnp.float32)).astype(jnp.bfloat16)
    last.wait_send()

    def drain(j, _):
        for p in range(pieces):
            i = j * pieces + p
            x_copy(i).wait_send()
            for d in range(1, ZN):
                z_copy(i, d).wait_send()
        for d in range(1, ZN):
            az_copy(j, d).wait_send()
        for d in range(ZN):
            ax_copy(j, d).wait_send()
        return 0
    lax.fori_loop(0, groups, drain, 0)


def fused(activations, qkv_weight, out_weight, key_cache, value_cache, lengths):
    rows_dev, context, groups, hd = key_cache.shape
    half_rows, depth = activations.shape
    rows = 2 * half_rows
    qkv_cols = qkv_weight.shape[1]
    heads_in = out_weight.shape[0]
    width = out_weight.shape[1]
    gq = heads_in // (groups * hd)
    block = (gq + 2) * hd
    pieces = 3
    piece = block // pieces
    n = groups * pieces
    bf16, f32 = jnp.bfloat16, jnp.float32

    half = hd // 2
    frequency = 500000.0 ** (-(jnp.arange(half).astype(f32) * 2.0 / hd))
    angles = lengths.astype(f32)[:, None] * frequency
    cosine, sine = jnp.cos(angles), jnp.sin(angles)
    cosine = jnp.concatenate([cosine, cosine], axis=1)
    sine = jnp.concatenate([-sine, sine], axis=1)
    limits = jnp.broadcast_to(jnp.repeat(lengths * groups, gq)[:, None], (rows_dev * gq, 128))

    anywhere = pl.BlockSpec(memory_space=pl.ANY)
    vmem = pl.BlockSpec(memory_space=pltpu.VMEM)
    dma = pltpu.SemaphoreType.DMA
    return pl.pallas_call(
        functools.partial(fused_kernel, (groups, gq, hd, piece, pieces, rows_dev)),
        out_shape=jax.ShapeDtypeStruct((half_rows, width), bf16),
        in_specs=[anywhere] * 5 + [vmem] * 3,
        out_specs=vmem,
        scratch_shapes=[
            pltpu.VMEM((rows, depth), bf16),
            pltpu.VMEM((SLOTS, depth, piece), bf16),
            pltpu.VMEM((heads_in, width), bf16),
            pltpu.VMEM((rows_dev, context * groups, hd), bf16),
            pltpu.VMEM((rows_dev, context * groups, hd), bf16),
            pltpu.VMEM((n, ZN, rows_dev, piece), f32),
            pltpu.VMEM((n, ZN, rows_dev, piece), f32),
            pltpu.VMEM((n, ZN, rows_dev, piece), f32),
            pltpu.VMEM((n, ZN, rows_dev, piece), f32),
            pltpu.VMEM((n, ZN - 1, rows_dev, piece), f32),
            pltpu.VMEM((rows_dev, block), f32),
            pltpu.VMEM((gq * rows_dev, hd), f32),
            pltpu.VMEM((gq * rows_dev, context * groups), f32),
            pltpu.VMEM((gq * rows_dev, hd), f32),
            pltpu.VMEM((groups, XN * ZN, gq * rows_dev, hd), bf16),
            pltpu.VMEM((rows, gq * hd), bf16),
            pltpu.VMEM((rows, width), f32),
            pltpu.VMEM((half_rows, width), bf16),
            pltpu.VMEM((half_rows, width), bf16),
            dma((3,)), dma((SLOTS,)), dma((groups,)), dma((2,)),
            dma((n,)), dma((n,)), dma((n, ZN - 1)), dma((n, ZN - 1)),
            dma((groups, ZN - 1)), dma((groups, ZN - 1)), dma((groups, ZN)), dma((groups, ZN)),
            dma, dma,
        ],
        compiler_params=pltpu.CompilerParams(
            collective_id=0, has_side_effects=True, vmem_limit_bytes=63 * 1024 * 1024),
        cost_estimate=pl.CostEstimate(
            flops=2 * rows * (depth * qkv_cols + heads_in * width),
            bytes_accessed=2 * (depth * qkv_cols + heads_in * width), transcendentals=0),
        name="fused_attention",
    )(
        activations, qkv_weight, out_weight,
        key_cache.reshape(rows_dev, context * groups, hd),
        value_cache.reshape(rows_dev, context * groups, hd),
        cosine, sine, limits,
    )


def rotate(vectors, positions):
    half_dim = vectors.shape[-1] // 2
    frequency = 500000.0 ** (-(jnp.arange(half_dim).astype(jnp.float32) * 2.0 / vectors.shape[-1]))
    angles = positions.astype(jnp.float32)[..., None] * frequency
    cosine = jnp.cos(angles)
    sine_part = jnp.sin(angles)
    lower_half = vectors[..., :half_dim]
    upper_half = vectors[..., half_dim:]
    return jnp.concatenate(
        [
            lower_half * cosine - upper_half * sine_part,
            upper_half * cosine + lower_half * sine_part,
        ],
        axis=-1,
    )


def attend(queries, new_key, new_value, keys, values, lengths):
    queries = rotate(queries.astype(jnp.float32), lengths[:, None, None]).astype(jnp.bfloat16)
    new_key = rotate(new_key.astype(jnp.float32), lengths[:, None]).astype(jnp.bfloat16)
    scaling = queries.shape[-1] ** (-0.5)
    scores = (
        jnp.einsum("rgqd,rpgd->rgqp", queries, keys, preferred_element_type=jnp.float32) * scaling
    )
    own_score = (
        jnp.einsum("rgqd,rgd->rgq", queries, new_key, preferred_element_type=jnp.float32) * scaling
    )
    visible = (jnp.arange(keys.shape[1])[None, :] < lengths[:, None])[:, None, None, :]
    masked = jnp.where(visible, scores, -1e30)
    highest = jnp.maximum(jnp.max(masked, axis=-1), own_score)
    raised = jnp.where(visible, jnp.exp(masked - highest[..., None]), 0.0)
    own_raised = jnp.exp(own_score - highest)
    denominator = jnp.sum(raised, axis=-1) + own_raised
    weights = (raised / denominator[..., None]).astype(jnp.bfloat16)
    own_weight = (own_raised / denominator).astype(jnp.bfloat16)
    blended = jnp.einsum("rgqp,rpgd->rgqd", weights, values, preferred_element_type=jnp.float32)
    blended = (
        blended
        + own_weight.astype(jnp.float32)[..., None] * new_value.astype(jnp.float32)[:, :, None, :]
    )
    return blended.astype(jnp.bfloat16)


def local(activations, qkv_weight, out_weight, key_cache, value_cache, lengths):
    rows_dev = key_cache.shape[0]
    head_groups = key_cache.shape[2]
    head_dim = key_cache.shape[3]
    all_rows = lax.all_gather(activations, "gy", axis=0, tiled=True)
    summed = lax.psum_scatter(
        jnp.dot(all_rows, qkv_weight, preferred_element_type=jnp.float32),
        "gx",
        scatter_dimension=0,
        tiled=True,
    )
    projected = summed.astype(jnp.bfloat16).reshape(rows_dev, head_groups, -1, head_dim)
    attended = attend(
        projected[:, :, :-2],
        projected[:, :, -2],
        projected[:, :, -1],
        key_cache,
        value_cache,
        lengths,
    )
    attended = attended.reshape(rows_dev, -1)
    partial_out = jnp.dot(
        lax.all_gather(attended, "gx", axis=0, tiled=True),
        out_weight,
        preferred_element_type=jnp.float32,
    )
    return lax.psum_scatter(partial_out.astype(jnp.bfloat16), "gy", scatter_dimension=0, tiled=True)


def solution(mesh):
    placed = (
        P(("groups", "gy"), "gx"),
        P("gx", "gy"),
        P("gy", "gx"),
        P(("groups", "gx"), None, "gy", None),
        P(("groups", "gx"), None, "gy", None),
        P(("groups", "gx")),
    )
    chosen = fused if mesh.shape["gx"] == XN * ZN and mesh.shape["gy"] == 2 else local
    return jax.shard_map(
        chosen, mesh=mesh, in_specs=placed, out_specs=P(("groups", "gy"), "gx"), check_vma=False
    )
```

```python
import functools
import math

import jax
import jax.numpy as jnp
from jax import lax
from jax.experimental import pallas as pl
from jax.experimental.pallas import tpu as pltpu
from jax.sharding import PartitionSpec as P

MESH = pl.DeviceIdType.MESH
XN, ZN = 2, 4
TILE = 256
SLOTS = 4


def fused_kernel(
    dims, act_hbm, wq_hbm, wo_hbm, key_hbm, val_hbm, len_ref, out_ref,
    act, wbuf, wo, keys, vals, xsend, xkeep, xrecv, zbuf, zrecv, proj, qrows, score, orows, split, cos_ref, sin_ref,
    att, lhs, acc, psend, precv,
    act_sem, w_sem, wo_sem, kv_sem, xs_sem, xr_sem, zs_sem, zr_sem,
    azs_sem, azr_sem, axs_sem, axr_sem, ps_sem, pr_sem,
):
    groups, gq, hd, piece, pieces, rows_dev = dims
    rows = act.shape[0]
    half_rows = rows // 2
    gx = lax.axis_index("gx")
    gy = lax.axis_index("gy")
    x = lax.rem(gx, XN)
    z = lax.div(gx, XN)
    xpeer = z * XN + (1 - x)
    ypeer = 1 - gy

    def zpeer(d):
        return lax.rem(z + d, ZN) * XN + x

    def zfrom(d):
        return lax.rem(z + ZN - d, ZN) * XN + x

    def w_copy(i):
        cols = pl.ds(pl.multiple_of(i * piece, piece), piece)
        slot = lax.rem(i, SLOTS)
        return pltpu.make_async_copy(wq_hbm.at[:, cols], wbuf.at[slot], w_sem.at[slot])

    group_width = gq * hd

    def wo_copy(j):
        part = pl.ds(pl.multiple_of(j * group_width, group_width), group_width)
        return pltpu.make_async_copy(wo_hbm.at[part], wo.at[part], wo_sem.at[j])

    key_copy = pltpu.make_async_copy(key_hbm, keys, kv_sem.at[0])
    val_copy = pltpu.make_async_copy(val_hbm, vals, kv_sem.at[1])

    def x_copy(i):
        return pltpu.make_async_remote_copy(
            xsend.at[i], xrecv.at[i], xs_sem.at[i], xr_sem.at[i],
            device_id={"gx": xpeer}, device_id_type=MESH)

    def z_copy(i, d):
        return pltpu.make_async_remote_copy(
            zbuf.at[i, lax.rem(z + d, ZN)], zrecv.at[i, d - 1], zs_sem.at[i, d - 1],
            zr_sem.at[i, d - 1], device_id={"gx": zpeer(d)}, device_id_type=MESH)

    def az_copy(j, d):
        return pltpu.make_async_remote_copy(
            att.at[j, gx], att.at[j, gx], azs_sem.at[j, d - 1], azr_sem.at[j, d - 1],
            device_id={"gx": zpeer(d)}, device_id_type=MESH)

    def az_arrival(j, d):
        return pltpu.make_async_remote_copy(
            att.at[j, zfrom(d)], att.at[j, zfrom(d)], azs_sem.at[j, d - 1], azr_sem.at[j, d - 1],
            device_id={"gx": zpeer(d)}, device_id_type=MESH)

    def ax_copy(j, d):
        return pltpu.make_async_remote_copy(
            att.at[j, zfrom(d)], att.at[j, zfrom(d)], axs_sem.at[j, d], axr_sem.at[j, d],
            device_id={"gx": xpeer}, device_id_type=MESH)

    def ax_arrival(j, d):
        block = lax.rem(z + ZN - d, ZN) * XN + (1 - x)
        return pltpu.make_async_remote_copy(
            att.at[j, block], att.at[j, block], axs_sem.at[j, d], axr_sem.at[j, d],
            device_id={"gx": xpeer}, device_id_type=MESH)

    for i in range(SLOTS):
        w_copy(i).start()
    mine = pl.ds(pl.multiple_of(gy * half_rows, half_rows), half_rows)
    theirs = pl.ds(pl.multiple_of(ypeer * half_rows, half_rows), half_rows)
    own_act = pltpu.make_async_copy(act_hbm, act.at[mine], act_sem.at[0])
    own_act.start()

    barrier = pltpu.get_barrier_semaphore()
    for d in range(1, ZN):
        pl.semaphore_signal(barrier, inc=1, device_id={"gx": zpeer(d)}, device_id_type=MESH)
    pl.semaphore_signal(barrier, inc=1, device_id={"gx": xpeer}, device_id_type=MESH)
    pl.semaphore_signal(barrier, inc=1, device_id={"gy": ypeer}, device_id_type=MESH)
    pl.semaphore_wait(barrier, ZN + 1)

    peer_act = pltpu.make_async_remote_copy(
        act_hbm, act.at[mine], act_sem.at[1], act_sem.at[2],
        device_id={"gy": ypeer}, device_id_type=MESH)
    peer_act.start()
    key_copy.start()
    val_copy.start()
    acc[...] = jnp.zeros_like(acc)
    row = lax.broadcasted_iota(jnp.int32, cos_ref.shape, 0)
    lane = lax.broadcasted_iota(jnp.int32, cos_ref.shape, 1)
    position = jnp.zeros(cos_ref.shape, jnp.int32)
    for r in range(rows_dev):
        position = jnp.where(row == r, len_ref[r], position)
    index = lax.rem(lane, hd // 2).astype(jnp.float32)
    angle = position.astype(jnp.float32) * jnp.exp(index * (-2.0 * math.log(500000.0) / hd))
    cos_ref[...] = jnp.cos(angle)
    sin_ref[...] = jnp.where(lane < hd // 2, -1.0, 1.0) * jnp.sin(angle)
    own_act.wait()
    peer_act.wait()

    def project(j):
        def one(p, _):
            i = j * pieces + p
            slot = lax.rem(i, SLOTS)
            w_copy(i).wait()
            for t in range(piece // TILE):
                cols = pl.ds(t * TILE, TILE)
                part = jnp.dot(act[...], wbuf[slot, :, cols], preferred_element_type=jnp.float32)
                part = part.reshape(ZN, XN, rows_dev, TILE)
                first, second = part[:, 0], part[:, 1]
                xkeep[i, :, :, cols] = jnp.where(x == 0, first, second)
                xsend[i, :, :, cols] = jnp.where(x == 0, second, first)
            x_copy(i).start()

            @pl.when(i + SLOTS < groups * pieces)
            def _():
                w_copy(i + SLOTS).start()
            return 0
        lax.fori_loop(0, pieces, one, 0)
        wo_copy(j).start()

    def across_x(j):
        def one(p, _):
            i = j * pieces + p
            x_copy(i).wait_recv()
            zbuf[i] = xkeep[i] + xrecv[i]
            for d in range(1, ZN):
                z_copy(i, d).start()
            return 0
        lax.fori_loop(0, pieces, one, 0)

    def separate():
        key_copy.wait()
        val_copy.wait()

        def one(r, _):
            for cache in (keys, vals):
                split[...] = cache[r].astype(jnp.float32)
                context = split.shape[0] // groups
                for g in range(groups):
                    cache[r, g * context:(g + 1) * context, :] = split[
                        pl.ds(g, context, stride=groups), :].astype(jnp.bfloat16)
            return 0
        lax.fori_loop(0, rows_dev, one, 0)

    def attention(j):
        for p in range(pieces):
            i = j * pieces + p
            for d in range(1, ZN):
                z_copy(i, d).wait_recv()
            total = zbuf[i, z] + zrecv[i, 0] + zrecv[i, 1] + zrecv[i, 2]
            proj[:, p * piece:(p + 1) * piece] = total.astype(jnp.bfloat16).astype(jnp.float32)

        def turned(h):
            v = proj[:, h * hd:(h + 1) * hd]
            swapped = jnp.concatenate([v[:, hd // 2:], v[:, :hd // 2]], axis=1)
            r = v * cos_ref[...] + swapped * sin_ref[...]
            return r.astype(jnp.bfloat16).astype(jnp.float32)

        for h in range(gq):
            qrows[h * rows_dev:(h + 1) * rows_dev, :] = turned(h)
        new_key = turned(gq)
        new_value = proj[:, (gq + 1) * hd:(gq + 2) * hd]
        scaling = hd ** -0.5
        own = []
        context = score.shape[1]
        mine_keys = pl.ds(pl.multiple_of(j * context, context), context)
        column = lax.broadcasted_iota(jnp.int32, (gq, context), 1)
        for r in range(rows_dev):
            q = qrows[pl.ds(r, gq, stride=rows_dev), :]
            seen = lax.dot_general(
                q.astype(jnp.bfloat16), keys[r, mine_keys], (((1,), (1,)), ((), ())),
                preferred_element_type=jnp.float32) * scaling
            score[r * gq:(r + 1) * gq, :] = jnp.where(column < len_ref[r], seen, -1e30)
            own.append(jnp.sum(q * new_key[r:r + 1, :], axis=1, keepdims=True) * scaling)
        own = jnp.concatenate(own, axis=0)
        masked = score[...]
        highest = jnp.maximum(jnp.max(masked, axis=1, keepdims=True), own)
        raised = jnp.exp(masked - highest)
        own_raised = jnp.exp(own - highest)
        inverse = 1.0 / (jnp.sum(raised, axis=1, keepdims=True) + own_raised)
        weights = (raised * inverse).astype(jnp.bfloat16)
        own_weight = (own_raised * inverse).astype(jnp.bfloat16).astype(jnp.float32)
        for r in range(rows_dev):
            part = slice(r * gq, (r + 1) * gq)
            blended = jnp.dot(weights[part], vals[r, mine_keys], preferred_element_type=jnp.float32)
            orows[pl.ds(r, gq, stride=rows_dev), :] = blended + own_weight[part] * new_value[r:r + 1, :]
        att[j, gx] = orows[...].astype(jnp.bfloat16)
        for d in range(1, ZN):
            az_copy(j, d).start()
        ax_copy(j, 0).start()

    def relay(j):
        for d in range(1, ZN):
            az_arrival(j, d).wait_recv()
            ax_copy(j, d).start()

    def output(j):
        for d in range(ZN):
            ax_arrival(j, d).wait_recv()
        for b in range(XN * ZN // 2):
            pair = []
            for s in range(2):
                block = att[j, 2 * b + s].astype(jnp.float32)
                pair.append(jnp.concatenate(
                    [block[h * rows_dev:(h + 1) * rows_dev] for h in range(gq)], axis=1))
            lhs[2 * b * rows_dev:2 * (b + 1) * rows_dev, :] = jnp.concatenate(
                pair, axis=0).astype(jnp.bfloat16)
        wo_copy(j).wait()
        depth = pl.ds(pl.multiple_of(j * group_width, group_width), group_width)

        def one(n, _):
            cols = pl.ds(pl.multiple_of(n * TILE, TILE), TILE)
            acc[:, cols] += jnp.dot(lhs[...], wo[depth, cols], preferred_element_type=jnp.float32)
            return 0
        lax.fori_loop(0, acc.shape[1] // TILE, one, 0)

    def step(t, _):
        for delay, stage in enumerate((project, across_x, attention, relay, output)):
            if delay == 1:
                pl.when(t == 1)(separate)

            @pl.when((t >= delay) & (t < groups + delay))
            def _(stage=stage, delay=delay):
                stage(t - delay)
        return 0
    lax.fori_loop(0, groups + 4, step, 0)

    psend[...] = acc[theirs, :].astype(jnp.bfloat16)
    last = pltpu.make_async_remote_copy(
        psend, precv, ps_sem, pr_sem, device_id={"gy": ypeer}, device_id_type=MESH)
    last.start()
    last.wait_recv()
    out_ref[...] = (acc[mine, :] + precv[...].astype(jnp.float32)).astype(jnp.bfloat16)
    last.wait_send()

    def drain(j, _):
        for p in range(pieces):
            i = j * pieces + p
            x_copy(i).wait_send()
            for d in range(1, ZN):
                z_copy(i, d).wait_send()
        for d in range(1, ZN):
            az_copy(j, d).wait_send()
        for d in range(ZN):
            ax_copy(j, d).wait_send()
        return 0
    lax.fori_loop(0, groups, drain, 0)


def fused(activations, qkv_weight, out_weight, key_cache, value_cache, lengths):
    rows_dev, context, groups, hd = key_cache.shape
    half_rows, depth = activations.shape
    rows = 2 * half_rows
    qkv_cols = qkv_weight.shape[1]
    heads_in = out_weight.shape[0]
    width = out_weight.shape[1]
    gq = heads_in // (groups * hd)
    block = (gq + 2) * hd
    pieces = 3
    piece = block // pieces
    n = groups * pieces
    bf16, f32 = jnp.bfloat16, jnp.float32

    anywhere = pl.BlockSpec(memory_space=pl.ANY)
    vmem = pl.BlockSpec(memory_space=pltpu.VMEM)
    dma = pltpu.SemaphoreType.DMA
    return pl.pallas_call(
        functools.partial(fused_kernel, (groups, gq, hd, piece, pieces, rows_dev)),
        out_shape=jax.ShapeDtypeStruct((half_rows, width), bf16),
        in_specs=[anywhere] * 5 + [pl.BlockSpec(memory_space=pltpu.SMEM)],
        out_specs=vmem,
        scratch_shapes=[
            pltpu.VMEM((rows, depth), bf16),
            pltpu.VMEM((SLOTS, depth, piece), bf16),
            pltpu.VMEM((heads_in, width), bf16),
            pltpu.VMEM((rows_dev, context * groups, hd), bf16),
            pltpu.VMEM((rows_dev, context * groups, hd), bf16),
            pltpu.VMEM((n, ZN, rows_dev, piece), f32),
            pltpu.VMEM((n, ZN, rows_dev, piece), f32),
            pltpu.VMEM((n, ZN, rows_dev, piece), f32),
            pltpu.VMEM((n, ZN, rows_dev, piece), f32),
            pltpu.VMEM((n, ZN - 1, rows_dev, piece), f32),
            pltpu.VMEM((rows_dev, block), f32),
            pltpu.VMEM((gq * rows_dev, hd), f32),
            pltpu.VMEM((gq * rows_dev, context), f32),
            pltpu.VMEM((gq * rows_dev, hd), f32),
            pltpu.VMEM((context * groups, hd), f32),
            pltpu.VMEM((rows_dev, hd), f32),
            pltpu.VMEM((rows_dev, hd), f32),
            pltpu.VMEM((groups, XN * ZN, gq * rows_dev, hd), bf16),
            pltpu.VMEM((rows, gq * hd), bf16),
            pltpu.VMEM((rows, width), f32),
            pltpu.VMEM((half_rows, width), bf16),
            pltpu.VMEM((half_rows, width), bf16),
            dma((3,)), dma((SLOTS,)), dma((groups,)), dma((2,)),
            dma((n,)), dma((n,)), dma((n, ZN - 1)), dma((n, ZN - 1)),
            dma((groups, ZN - 1)), dma((groups, ZN - 1)), dma((groups, ZN)), dma((groups, ZN)),
            dma, dma,
        ],
        compiler_params=pltpu.CompilerParams(
            collective_id=0, has_side_effects=True, vmem_limit_bytes=63 * 1024 * 1024),
        cost_estimate=pl.CostEstimate(
            flops=2 * rows * (depth * qkv_cols + heads_in * width),
            bytes_accessed=2 * (depth * qkv_cols + heads_in * width), transcendentals=0),
        name="fused_attention",
    )(
        activations, qkv_weight, out_weight,
        key_cache.reshape(rows_dev, context * groups, hd),
        value_cache.reshape(rows_dev, context * groups, hd),
        lengths,
    )


def rotate(vectors, positions):
    half_dim = vectors.shape[-1] // 2
    frequency = 500000.0 ** (-(jnp.arange(half_dim).astype(jnp.float32) * 2.0 / vectors.shape[-1]))
    angles = positions.astype(jnp.float32)[..., None] * frequency
    cosine = jnp.cos(angles)
    sine_part = jnp.sin(angles)
    lower_half = vectors[..., :half_dim]
    upper_half = vectors[..., half_dim:]
    return jnp.concatenate(
        [
            lower_half * cosine - upper_half * sine_part,
            upper_half * cosine + lower_half * sine_part,
        ],
        axis=-1,
    )


def attend(queries, new_key, new_value, keys, values, lengths):
    queries = rotate(queries.astype(jnp.float32), lengths[:, None, None]).astype(jnp.bfloat16)
    new_key = rotate(new_key.astype(jnp.float32), lengths[:, None]).astype(jnp.bfloat16)
    scaling = queries.shape[-1] ** (-0.5)
    scores = (
        jnp.einsum("rgqd,rpgd->rgqp", queries, keys, preferred_element_type=jnp.float32) * scaling
    )
    own_score = (
        jnp.einsum("rgqd,rgd->rgq", queries, new_key, preferred_element_type=jnp.float32) * scaling
    )
    visible = (jnp.arange(keys.shape[1])[None, :] < lengths[:, None])[:, None, None, :]
    masked = jnp.where(visible, scores, -1e30)
    highest = jnp.maximum(jnp.max(masked, axis=-1), own_score)
    raised = jnp.where(visible, jnp.exp(masked - highest[..., None]), 0.0)
    own_raised = jnp.exp(own_score - highest)
    denominator = jnp.sum(raised, axis=-1) + own_raised
    weights = (raised / denominator[..., None]).astype(jnp.bfloat16)
    own_weight = (own_raised / denominator).astype(jnp.bfloat16)
    blended = jnp.einsum("rgqp,rpgd->rgqd", weights, values, preferred_element_type=jnp.float32)
    blended = (
        blended
        + own_weight.astype(jnp.float32)[..., None] * new_value.astype(jnp.float32)[:, :, None, :]
    )
    return blended.astype(jnp.bfloat16)


def local(activations, qkv_weight, out_weight, key_cache, value_cache, lengths):
    rows_dev = key_cache.shape[0]
    head_groups = key_cache.shape[2]
    head_dim = key_cache.shape[3]
    all_rows = lax.all_gather(activations, "gy", axis=0, tiled=True)
    summed = lax.psum_scatter(
        jnp.dot(all_rows, qkv_weight, preferred_element_type=jnp.float32),
        "gx",
        scatter_dimension=0,
        tiled=True,
    )
    projected = summed.astype(jnp.bfloat16).reshape(rows_dev, head_groups, -1, head_dim)
    attended = attend(
        projected[:, :, :-2],
        projected[:, :, -2],
        projected[:, :, -1],
        key_cache,
        value_cache,
        lengths,
    )
    attended = attended.reshape(rows_dev, -1)
    partial_out = jnp.dot(
        lax.all_gather(attended, "gx", axis=0, tiled=True),
        out_weight,
        preferred_element_type=jnp.float32,
    )
    return lax.psum_scatter(partial_out.astype(jnp.bfloat16), "gy", scatter_dimension=0, tiled=True)


def solution(mesh):
    placed = (
        P(("groups", "gy"), "gx"),
        P("gx", "gy"),
        P("gy", "gx"),
        P(("groups", "gx"), None, "gy", None),
        P(("groups", "gx"), None, "gy", None),
        P(("groups", "gx")),
    )
    chosen = fused if mesh.shape["gx"] == XN * ZN and mesh.shape["gy"] == 2 else local
    return jax.shard_map(
        chosen, mesh=mesh, in_specs=placed, out_specs=P(("groups", "gy"), "gx"), check_vma=False
    )
```

```python
import functools
import math

import jax
import jax.numpy as jnp
from jax import lax
from jax.experimental import pallas as pl
from jax.experimental.pallas import tpu as pltpu
from jax.sharding import PartitionSpec as P

MESH = pl.DeviceIdType.MESH
XN, ZN = 2, 4
TILE = 256
SLOTS = 4


def fused_kernel(
    dims, act_hbm, wq_hbm, wo_hbm, key_hbm, val_hbm, len_ref, out_ref,
    act, wbuf, wo, keys, vals, xsend, xkeep, xrecv, zbuf, znear, zsum, zfar, proj, qrows, score, orows, split, cos_ref, sin_ref,
    att, lhs, acc, psend, precv,
    act_sem, w_sem, wo_sem, kv_sem, xs_sem, xr_sem, ns_sem, nr_sem, fs_sem, fr_sem,
    azs_sem, azr_sem, axs_sem, axr_sem, ps_sem, pr_sem,
):
    groups, gq, hd, piece, pieces, rows_dev = dims
    rows = act.shape[0]
    half_rows = rows // 2
    gx = lax.axis_index("gx")
    gy = lax.axis_index("gy")
    x = lax.rem(gx, XN)
    z = lax.div(gx, XN)
    xpeer = z * XN + (1 - x)
    ypeer = 1 - gy
    low = lax.rem(z, 2)
    high = lax.div(z, 2)

    def zpeer(d):
        return lax.rem(z + d, ZN) * XN + x

    def zfrom(d):
        return lax.rem(z + ZN - d, ZN) * XN + x

    def w_copy(i):
        cols = pl.ds(pl.multiple_of(i * piece, piece), piece)
        slot = lax.rem(i, SLOTS)
        return pltpu.make_async_copy(wq_hbm.at[:, cols], wbuf.at[slot], w_sem.at[slot])

    group_width = gq * hd

    def wo_copy(j):
        part = pl.ds(pl.multiple_of(j * group_width, group_width), group_width)
        return pltpu.make_async_copy(wo_hbm.at[part], wo.at[part], wo_sem.at[j])

    key_copy = pltpu.make_async_copy(key_hbm, keys, kv_sem.at[0])
    val_copy = pltpu.make_async_copy(val_hbm, vals, kv_sem.at[1])

    def x_copy(i):
        return pltpu.make_async_remote_copy(
            xsend.at[i], xrecv.at[i], xs_sem.at[i], xr_sem.at[i],
            device_id={"gx": xpeer}, device_id_type=MESH)

    def near_copy(i):
        return pltpu.make_async_remote_copy(
            zbuf.at[i, 1 - low], znear.at[i], ns_sem.at[i], nr_sem.at[i],
            device_id={"gx": (2 * high + 1 - low) * XN + x}, device_id_type=MESH)

    def far_copy(i):
        return pltpu.make_async_remote_copy(
            zsum.at[i, 1 - high], zfar.at[i], fs_sem.at[i], fr_sem.at[i],
            device_id={"gx": (2 * (1 - high) + low) * XN + x}, device_id_type=MESH)

    def az_copy(j, d):
        return pltpu.make_async_remote_copy(
            att.at[j, gx], att.at[j, gx], azs_sem.at[j, d - 1], azr_sem.at[j, d - 1],
            device_id={"gx": zpeer(d)}, device_id_type=MESH)

    def az_arrival(j, d):
        return pltpu.make_async_remote_copy(
            att.at[j, zfrom(d)], att.at[j, zfrom(d)], azs_sem.at[j, d - 1], azr_sem.at[j, d - 1],
            device_id={"gx": zpeer(d)}, device_id_type=MESH)

    def ax_copy(j, d):
        return pltpu.make_async_remote_copy(
            att.at[j, zfrom(d)], att.at[j, zfrom(d)], axs_sem.at[j, d], axr_sem.at[j, d],
            device_id={"gx": xpeer}, device_id_type=MESH)

    def ax_arrival(j, d):
        block = lax.rem(z + ZN - d, ZN) * XN + (1 - x)
        return pltpu.make_async_remote_copy(
            att.at[j, block], att.at[j, block], axs_sem.at[j, d], axr_sem.at[j, d],
            device_id={"gx": xpeer}, device_id_type=MESH)

    for i in range(SLOTS):
        w_copy(i).start()
    mine = pl.ds(pl.multiple_of(gy * half_rows, half_rows), half_rows)
    theirs = pl.ds(pl.multiple_of(ypeer * half_rows, half_rows), half_rows)
    own_act = pltpu.make_async_copy(act_hbm, act.at[mine], act_sem.at[0])
    own_act.start()

    barrier = pltpu.get_barrier_semaphore()
    for d in range(1, ZN):
        pl.semaphore_signal(barrier, inc=1, device_id={"gx": zpeer(d)}, device_id_type=MESH)
    pl.semaphore_signal(barrier, inc=1, device_id={"gx": xpeer}, device_id_type=MESH)
    pl.semaphore_signal(barrier, inc=1, device_id={"gy": ypeer}, device_id_type=MESH)
    pl.semaphore_wait(barrier, ZN + 1)

    peer_act = pltpu.make_async_remote_copy(
        act_hbm, act.at[mine], act_sem.at[1], act_sem.at[2],
        device_id={"gy": ypeer}, device_id_type=MESH)
    peer_act.start()
    key_copy.start()
    val_copy.start()
    acc[...] = jnp.zeros_like(acc)
    row = lax.broadcasted_iota(jnp.int32, cos_ref.shape, 0)
    lane = lax.broadcasted_iota(jnp.int32, cos_ref.shape, 1)
    position = jnp.zeros(cos_ref.shape, jnp.int32)
    for r in range(rows_dev):
        position = jnp.where(row == r, len_ref[r], position)
    index = lax.rem(lane, hd // 2).astype(jnp.float32)
    angle = position.astype(jnp.float32) * jnp.exp(index * (-2.0 * math.log(500000.0) / hd))
    cos_ref[...] = jnp.cos(angle)
    sin_ref[...] = jnp.where(lane < hd // 2, -1.0, 1.0) * jnp.sin(angle)
    own_act.wait()
    peer_act.wait()

    def project(j):
        def one(p, _):
            i = j * pieces + p
            slot = lax.rem(i, SLOTS)
            w_copy(i).wait()
            for t in range(piece // TILE):
                cols = pl.ds(t * TILE, TILE)
                part = jnp.dot(act[...], wbuf[slot, :, cols], preferred_element_type=jnp.float32)
                part = part.reshape(ZN, XN, rows_dev, TILE)
                first, second = part[:, 0], part[:, 1]
                xkeep[i, :, :, cols] = jnp.where(x == 0, first, second)
                xsend[i, :, :, cols] = jnp.where(x == 0, second, first)
            x_copy(i).start()

            @pl.when(i + SLOTS < groups * pieces)
            def _():
                w_copy(i + SLOTS).start()
            return 0
        lax.fori_loop(0, pieces, one, 0)
        wo_copy(j).start()

    def across_x(j):
        def one(p, _):
            i = j * pieces + p
            x_copy(i).wait_recv()
            for b in range(ZN):
                zbuf[i, b % 2, b // 2] = xkeep[i, b] + xrecv[i, b]
            near_copy(i).start()
            return 0
        lax.fori_loop(0, pieces, one, 0)

    def across_z(j):
        def one(p, _):
            i = j * pieces + p
            near_copy(i).wait_recv()
            zsum[i] = zbuf[i, low] + znear[i]
            far_copy(i).start()
            return 0
        lax.fori_loop(0, pieces, one, 0)

    def separate():
        key_copy.wait()
        val_copy.wait()

        def one(r, _):
            for cache in (keys, vals):
                split[...] = cache[r].astype(jnp.float32)
                context = split.shape[0] // groups
                for g in range(groups):
                    cache[r, g * context:(g + 1) * context, :] = split[
                        pl.ds(g, context, stride=groups), :].astype(jnp.bfloat16)
            return 0
        lax.fori_loop(0, rows_dev, one, 0)

    def attention(j):
        for p in range(pieces):
            i = j * pieces + p
            far_copy(i).wait_recv()
            total = zsum[i, high] + zfar[i]
            proj[:, p * piece:(p + 1) * piece] = total.astype(jnp.bfloat16).astype(jnp.float32)

        def turned(h):
            v = proj[:, h * hd:(h + 1) * hd]
            swapped = jnp.concatenate([v[:, hd // 2:], v[:, :hd // 2]], axis=1)
            r = v * cos_ref[...] + swapped * sin_ref[...]
            return r.astype(jnp.bfloat16).astype(jnp.float32)

        for h in range(gq):
            qrows[h * rows_dev:(h + 1) * rows_dev, :] = turned(h)
        new_key = turned(gq)
        new_value = proj[:, (gq + 1) * hd:(gq + 2) * hd]
        scaling = hd ** -0.5
        own = []
        context = score.shape[1]
        mine_keys = pl.ds(pl.multiple_of(j * context, context), context)
        column = lax.broadcasted_iota(jnp.int32, (gq, context), 1)
        for r in range(rows_dev):
            q = qrows[pl.ds(r, gq, stride=rows_dev), :]
            seen = lax.dot_general(
                q.astype(jnp.bfloat16), keys[r, mine_keys], (((1,), (1,)), ((), ())),
                preferred_element_type=jnp.float32) * scaling
            score[r * gq:(r + 1) * gq, :] = jnp.where(column < len_ref[r], seen, -1e30)
            own.append(jnp.sum(q * new_key[r:r + 1, :], axis=1, keepdims=True) * scaling)
        own = jnp.concatenate(own, axis=0)
        masked = score[...]
        highest = jnp.maximum(jnp.max(masked, axis=1, keepdims=True), own)
        raised = jnp.exp(masked - highest)
        own_raised = jnp.exp(own - highest)
        inverse = 1.0 / (jnp.sum(raised, axis=1, keepdims=True) + own_raised)
        weights = (raised * inverse).astype(jnp.bfloat16)
        own_weight = (own_raised * inverse).astype(jnp.bfloat16).astype(jnp.float32)
        for r in range(rows_dev):
            part = slice(r * gq, (r + 1) * gq)
            blended = jnp.dot(weights[part], vals[r, mine_keys], preferred_element_type=jnp.float32)
            orows[pl.ds(r, gq, stride=rows_dev), :] = blended + own_weight[part] * new_value[r:r + 1, :]
        att[j, gx] = orows[...].astype(jnp.bfloat16)
        for d in range(1, ZN):
            az_copy(j, d).start()
        ax_copy(j, 0).start()

    def relay(j):
        for d in range(1, ZN):
            az_arrival(j, d).wait_recv()
            ax_copy(j, d).start()

    def output(j):
        for d in range(ZN):
            ax_arrival(j, d).wait_recv()
        for b in range(XN * ZN // 2):
            pair = []
            for s in range(2):
                block = att[j, 2 * b + s].astype(jnp.float32)
                pair.append(jnp.concatenate(
                    [block[h * rows_dev:(h + 1) * rows_dev] for h in range(gq)], axis=1))
            lhs[2 * b * rows_dev:2 * (b + 1) * rows_dev, :] = jnp.concatenate(
                pair, axis=0).astype(jnp.bfloat16)
        wo_copy(j).wait()
        depth = pl.ds(pl.multiple_of(j * group_width, group_width), group_width)

        def one(n, _):
            cols = pl.ds(pl.multiple_of(n * TILE, TILE), TILE)
            acc[:, cols] += jnp.dot(lhs[...], wo[depth, cols], preferred_element_type=jnp.float32)
            return 0
        lax.fori_loop(0, acc.shape[1] // TILE, one, 0)

    def step(t, _):
        for delay, stage in enumerate(
                (project, across_x, across_z, attention, relay, output)):
            if delay == 1:
                pl.when(t == 1)(separate)

            @pl.when((t >= delay) & (t < groups + delay))
            def _(stage=stage, delay=delay):
                stage(t - delay)
        return 0
    lax.fori_loop(0, groups + 5, step, 0)

    psend[...] = acc[theirs, :].astype(jnp.bfloat16)
    last = pltpu.make_async_remote_copy(
        psend, precv, ps_sem, pr_sem, device_id={"gy": ypeer}, device_id_type=MESH)
    last.start()
    last.wait_recv()
    out_ref[...] = (acc[mine, :] + precv[...].astype(jnp.float32)).astype(jnp.bfloat16)
    last.wait_send()

    def drain(j, _):
        for p in range(pieces):
            i = j * pieces + p
            x_copy(i).wait_send()
            near_copy(i).wait_send()
            far_copy(i).wait_send()
        for d in range(1, ZN):
            az_copy(j, d).wait_send()
        for d in range(ZN):
            ax_copy(j, d).wait_send()
        return 0
    lax.fori_loop(0, groups, drain, 0)


def fused(activations, qkv_weight, out_weight, key_cache, value_cache, lengths):
    rows_dev, context, groups, hd = key_cache.shape
    half_rows, depth = activations.shape
    rows = 2 * half_rows
    qkv_cols = qkv_weight.shape[1]
    heads_in = out_weight.shape[0]
    width = out_weight.shape[1]
    gq = heads_in // (groups * hd)
    block = (gq + 2) * hd
    pieces = 3
    piece = block // pieces
    n = groups * pieces
    bf16, f32 = jnp.bfloat16, jnp.float32

    anywhere = pl.BlockSpec(memory_space=pl.ANY)
    vmem = pl.BlockSpec(memory_space=pltpu.VMEM)
    dma = pltpu.SemaphoreType.DMA
    return pl.pallas_call(
        functools.partial(fused_kernel, (groups, gq, hd, piece, pieces, rows_dev)),
        out_shape=jax.ShapeDtypeStruct((half_rows, width), bf16),
        in_specs=[anywhere] * 5 + [pl.BlockSpec(memory_space=pltpu.SMEM)],
        out_specs=vmem,
        scratch_shapes=[
            pltpu.VMEM((rows, depth), bf16),
            pltpu.VMEM((SLOTS, depth, piece), bf16),
            pltpu.VMEM((heads_in, width), bf16),
            pltpu.VMEM((rows_dev, context * groups, hd), bf16),
            pltpu.VMEM((rows_dev, context * groups, hd), bf16),
            pltpu.VMEM((n, ZN, rows_dev, piece), f32),
            pltpu.VMEM((n, ZN, rows_dev, piece), f32),
            pltpu.VMEM((n, ZN, rows_dev, piece), f32),
            pltpu.VMEM((n, 2, ZN // 2, rows_dev, piece), f32),
            pltpu.VMEM((n, ZN // 2, rows_dev, piece), f32),
            pltpu.VMEM((n, ZN // 2, rows_dev, piece), f32),
            pltpu.VMEM((n, rows_dev, piece), f32),
            pltpu.VMEM((rows_dev, block), f32),
            pltpu.VMEM((gq * rows_dev, hd), f32),
            pltpu.VMEM((gq * rows_dev, context), f32),
            pltpu.VMEM((gq * rows_dev, hd), f32),
            pltpu.VMEM((context * groups, hd), f32),
            pltpu.VMEM((rows_dev, hd), f32),
            pltpu.VMEM((rows_dev, hd), f32),
            pltpu.VMEM((groups, XN * ZN, gq * rows_dev, hd), bf16),
            pltpu.VMEM((rows, gq * hd), bf16),
            pltpu.VMEM((rows, width), f32),
            pltpu.VMEM((half_rows, width), bf16),
            pltpu.VMEM((half_rows, width), bf16),
            dma((3,)), dma((SLOTS,)), dma((groups,)), dma((2,)),
            dma((n,)), dma((n,)), dma((n,)), dma((n,)), dma((n,)), dma((n,)),
            dma((groups, ZN - 1)), dma((groups, ZN - 1)), dma((groups, ZN)), dma((groups, ZN)),
            dma, dma,
        ],
        compiler_params=pltpu.CompilerParams(
            collective_id=0, has_side_effects=True, vmem_limit_bytes=63 * 1024 * 1024),
        cost_estimate=pl.CostEstimate(
            flops=2 * rows * (depth * qkv_cols + heads_in * width),
            bytes_accessed=2 * (depth * qkv_cols + heads_in * width), transcendentals=0),
        name="fused_attention",
    )(
        activations, qkv_weight, out_weight,
        key_cache.reshape(rows_dev, context * groups, hd),
        value_cache.reshape(rows_dev, context * groups, hd),
        lengths,
    )


def rotate(vectors, positions):
    half_dim = vectors.shape[-1] // 2
    frequency = 500000.0 ** (-(jnp.arange(half_dim).astype(jnp.float32) * 2.0 / vectors.shape[-1]))
    angles = positions.astype(jnp.float32)[..., None] * frequency
    cosine = jnp.cos(angles)
    sine_part = jnp.sin(angles)
    lower_half = vectors[..., :half_dim]
    upper_half = vectors[..., half_dim:]
    return jnp.concatenate(
        [
            lower_half * cosine - upper_half * sine_part,
            upper_half * cosine + lower_half * sine_part,
        ],
        axis=-1,
    )


def attend(queries, new_key, new_value, keys, values, lengths):
    queries = rotate(queries.astype(jnp.float32), lengths[:, None, None]).astype(jnp.bfloat16)
    new_key = rotate(new_key.astype(jnp.float32), lengths[:, None]).astype(jnp.bfloat16)
    scaling = queries.shape[-1] ** (-0.5)
    scores = (
        jnp.einsum("rgqd,rpgd->rgqp", queries, keys, preferred_element_type=jnp.float32) * scaling
    )
    own_score = (
        jnp.einsum("rgqd,rgd->rgq", queries, new_key, preferred_element_type=jnp.float32) * scaling
    )
    visible = (jnp.arange(keys.shape[1])[None, :] < lengths[:, None])[:, None, None, :]
    masked = jnp.where(visible, scores, -1e30)
    highest = jnp.maximum(jnp.max(masked, axis=-1), own_score)
    raised = jnp.where(visible, jnp.exp(masked - highest[..., None]), 0.0)
    own_raised = jnp.exp(own_score - highest)
    denominator = jnp.sum(raised, axis=-1) + own_raised
    weights = (raised / denominator[..., None]).astype(jnp.bfloat16)
    own_weight = (own_raised / denominator).astype(jnp.bfloat16)
    blended = jnp.einsum("rgqp,rpgd->rgqd", weights, values, preferred_element_type=jnp.float32)
    blended = (
        blended
        + own_weight.astype(jnp.float32)[..., None] * new_value.astype(jnp.float32)[:, :, None, :]
    )
    return blended.astype(jnp.bfloat16)


def local(activations, qkv_weight, out_weight, key_cache, value_cache, lengths):
    rows_dev = key_cache.shape[0]
    head_groups = key_cache.shape[2]
    head_dim = key_cache.shape[3]
    all_rows = lax.all_gather(activations, "gy", axis=0, tiled=True)
    summed = lax.psum_scatter(
        jnp.dot(all_rows, qkv_weight, preferred_element_type=jnp.float32),
        "gx",
        scatter_dimension=0,
        tiled=True,
    )
    projected = summed.astype(jnp.bfloat16).reshape(rows_dev, head_groups, -1, head_dim)
    attended = attend(
        projected[:, :, :-2],
        projected[:, :, -2],
        projected[:, :, -1],
        key_cache,
        value_cache,
        lengths,
    )
    attended = attended.reshape(rows_dev, -1)
    partial_out = jnp.dot(
        lax.all_gather(attended, "gx", axis=0, tiled=True),
        out_weight,
        preferred_element_type=jnp.float32,
    )
    return lax.psum_scatter(partial_out.astype(jnp.bfloat16), "gy", scatter_dimension=0, tiled=True)


def solution(mesh):
    placed = (
        P(("groups", "gy"), "gx"),
        P("gx", "gy"),
        P("gy", "gx"),
        P(("groups", "gx"), None, "gy", None),
        P(("groups", "gx"), None, "gy", None),
        P(("groups", "gx")),
    )
    chosen = fused if mesh.shape["gx"] == XN * ZN and mesh.shape["gy"] == 2 else local
    return jax.shard_map(
        chosen, mesh=mesh, in_specs=placed, out_specs=P(("groups", "gy"), "gx"), check_vma=False
    )
```

```python
import functools
import math

import jax
import jax.numpy as jnp
from jax import lax
from jax.experimental import pallas as pl
from jax.experimental.pallas import tpu as pltpu
from jax.sharding import PartitionSpec as P

MESH = pl.DeviceIdType.MESH
XN, ZN = 2, 4
TILE = 256
SLOTS = 4


def fused_kernel(
    dims, act_hbm, wq_hbm, wo_hbm, key_hbm, val_hbm, len_ref, out_ref,
    act, wbuf, wo, keys, vals, xsend, xkeep, xrecv, zbuf, zrecv, proj, qrows, score, orows, split, cos_ref, sin_ref,
    att, lhs, acc, psend, precv,
    act_sem, w_sem, wo_sem, kv_sem, xs_sem, xr_sem, zs_sem, zr_sem,
    azs_sem, azr_sem, axs_sem, axr_sem, ps_sem, pr_sem,
):
    groups, gq, hd, piece, pieces, rows_dev = dims
    rows = act.shape[0]
    half_rows = rows // 2
    gx = lax.axis_index("gx")
    gy = lax.axis_index("gy")
    x = lax.rem(gx, XN)
    z = lax.div(gx, XN)
    xpeer = z * XN + (1 - x)
    ypeer = 1 - gy

    def zpeer(d):
        return lax.rem(z + d, ZN) * XN + x

    def zfrom(d):
        return lax.rem(z + ZN - d, ZN) * XN + x

    def w_copy(i):
        cols = pl.ds(pl.multiple_of(i * piece, piece), piece)
        slot = lax.rem(i, SLOTS)
        return pltpu.make_async_copy(wq_hbm.at[:, cols], wbuf.at[slot], w_sem.at[slot])

    group_width = gq * hd

    def wo_copy(j):
        part = pl.ds(pl.multiple_of(j * group_width, group_width), group_width)
        return pltpu.make_async_copy(wo_hbm.at[part], wo.at[part], wo_sem.at[j])

    key_copy = pltpu.make_async_copy(key_hbm, keys, kv_sem.at[0])
    val_copy = pltpu.make_async_copy(val_hbm, vals, kv_sem.at[1])

    def x_copy(i):
        return pltpu.make_async_remote_copy(
            xsend.at[i], xrecv.at[i], xs_sem.at[i], xr_sem.at[i],
            device_id={"gx": xpeer}, device_id_type=MESH)

    def z_copy(i, d):
        return pltpu.make_async_remote_copy(
            zbuf.at[i, lax.rem(z + d, ZN)], zrecv.at[i, d - 1], zs_sem.at[i, d - 1],
            zr_sem.at[i, d - 1], device_id={"gx": zpeer(d)}, device_id_type=MESH)

    def az_copy(j, d):
        return pltpu.make_async_remote_copy(
            att.at[j, gx], att.at[j, gx], azs_sem.at[j, d - 1], azr_sem.at[j, d - 1],
            device_id={"gx": zpeer(d)}, device_id_type=MESH)

    def az_arrival(j, d):
        return pltpu.make_async_remote_copy(
            att.at[j, zfrom(d)], att.at[j, zfrom(d)], azs_sem.at[j, d - 1], azr_sem.at[j, d - 1],
            device_id={"gx": zpeer(d)}, device_id_type=MESH)

    def ax_copy(j, d):
        return pltpu.make_async_remote_copy(
            att.at[j, zfrom(d)], att.at[j, zfrom(d)], axs_sem.at[j, d], axr_sem.at[j, d],
            device_id={"gx": xpeer}, device_id_type=MESH)

    def ax_arrival(j, d):
        block = lax.rem(z + ZN - d, ZN) * XN + (1 - x)
        return pltpu.make_async_remote_copy(
            att.at[j, block], att.at[j, block], axs_sem.at[j, d], axr_sem.at[j, d],
            device_id={"gx": xpeer}, device_id_type=MESH)

    for i in range(SLOTS):
        w_copy(i).start()
    mine = pl.ds(pl.multiple_of(gy * half_rows, half_rows), half_rows)
    theirs = pl.ds(pl.multiple_of(ypeer * half_rows, half_rows), half_rows)
    own_act = pltpu.make_async_copy(act_hbm, act.at[mine], act_sem.at[0])
    own_act.start()

    barrier = pltpu.get_barrier_semaphore()
    for d in range(1, ZN):
        pl.semaphore_signal(barrier, inc=1, device_id={"gx": zpeer(d)}, device_id_type=MESH)
    pl.semaphore_signal(barrier, inc=1, device_id={"gx": xpeer}, device_id_type=MESH)
    pl.semaphore_signal(barrier, inc=1, device_id={"gy": ypeer}, device_id_type=MESH)
    pl.semaphore_wait(barrier, ZN + 1)

    peer_act = pltpu.make_async_remote_copy(
        act_hbm, act.at[mine], act_sem.at[1], act_sem.at[2],
        device_id={"gy": ypeer}, device_id_type=MESH)
    peer_act.start()
    key_copy.start()
    val_copy.start()
    acc[...] = jnp.zeros_like(acc)
    row = lax.broadcasted_iota(jnp.int32, cos_ref.shape, 0)
    lane = lax.broadcasted_iota(jnp.int32, cos_ref.shape, 1)
    position = jnp.zeros(cos_ref.shape, jnp.int32)
    for r in range(rows_dev):
        position = jnp.where(row == r, len_ref[r], position)
    index = lax.rem(lane, hd // 2).astype(jnp.float32)
    angle = position.astype(jnp.float32) * jnp.exp(index * (-2.0 * math.log(500000.0) / hd))
    cos_ref[...] = jnp.cos(angle)
    sin_ref[...] = jnp.where(lane < hd // 2, -1.0, 1.0) * jnp.sin(angle)
    own_act.wait()
    peer_act.wait()

    def project(j):
        def one(p, _):
            i = j * pieces + p
            slot = lax.rem(i, SLOTS)
            w_copy(i).wait()
            for t in range(piece // TILE):
                cols = pl.ds(t * TILE, TILE)
                part = jnp.dot(act[...], wbuf[slot, :, cols], preferred_element_type=jnp.float32)
                part = part.reshape(ZN, XN, rows_dev, TILE)
                first, second = part[:, 0], part[:, 1]
                xkeep[i, :, :, cols] = jnp.where(x == 0, first, second)
                xsend[i, :, :, cols] = jnp.where(x == 0, second, first)
            x_copy(i).start()

            @pl.when(i + SLOTS < groups * pieces)
            def _():
                w_copy(i + SLOTS).start()
            return 0
        lax.fori_loop(0, pieces, one, 0)

    def across_x(j):
        def one(p, _):
            i = j * pieces + p
            x_copy(i).wait_recv()
            zbuf[i] = xkeep[i] + xrecv[i]
            for d in range(1, ZN):
                z_copy(i, d).start()
            return 0
        lax.fori_loop(0, pieces, one, 0)

    def separate():
        key_copy.wait()
        val_copy.wait()

        def one(r, _):
            for cache in (keys, vals):
                split[...] = cache[r].astype(jnp.float32)
                context = split.shape[0] // groups
                for g in range(groups):
                    cache[r, g * context:(g + 1) * context, :] = split[
                        pl.ds(g, context, stride=groups), :].astype(jnp.bfloat16)
            return 0
        lax.fori_loop(0, rows_dev, one, 0)

    def attention(j):
        wo_copy(j).start()
        for p in range(pieces):
            i = j * pieces + p
            for d in range(1, ZN):
                z_copy(i, d).wait_recv()
            total = zbuf[i, z] + zrecv[i, 0] + zrecv[i, 1] + zrecv[i, 2]
            proj[:, p * piece:(p + 1) * piece] = total.astype(jnp.bfloat16).astype(jnp.float32)

        def turned(h):
            v = proj[:, h * hd:(h + 1) * hd]
            swapped = jnp.concatenate([v[:, hd // 2:], v[:, :hd // 2]], axis=1)
            r = v * cos_ref[...] + swapped * sin_ref[...]
            return r.astype(jnp.bfloat16).astype(jnp.float32)

        for h in range(gq):
            qrows[h * rows_dev:(h + 1) * rows_dev, :] = turned(h)
        new_key = turned(gq)
        new_value = proj[:, (gq + 1) * hd:(gq + 2) * hd]
        scaling = hd ** -0.5
        own = []
        context = score.shape[1]
        mine_keys = pl.ds(pl.multiple_of(j * context, context), context)
        column = lax.broadcasted_iota(jnp.int32, (gq, context), 1)
        for r in range(rows_dev):
            q = qrows[pl.ds(r, gq, stride=rows_dev), :]
            seen = lax.dot_general(
                q.astype(jnp.bfloat16), keys[r, mine_keys], (((1,), (1,)), ((), ())),
                preferred_element_type=jnp.float32) * scaling
            score[r * gq:(r + 1) * gq, :] = jnp.where(column < len_ref[r], seen, -1e30)
            own.append(jnp.sum(q * new_key[r:r + 1, :], axis=1, keepdims=True) * scaling)
        own = jnp.concatenate(own, axis=0)
        masked = score[...]
        highest = jnp.maximum(jnp.max(masked, axis=1, keepdims=True), own)
        raised = jnp.exp(masked - highest)
        own_raised = jnp.exp(own - highest)
        inverse = 1.0 / (jnp.sum(raised, axis=1, keepdims=True) + own_raised)
        weights = (raised * inverse).astype(jnp.bfloat16)
        own_weight = (own_raised * inverse).astype(jnp.bfloat16).astype(jnp.float32)
        for r in range(rows_dev):
            part = slice(r * gq, (r + 1) * gq)
            blended = jnp.dot(weights[part], vals[r, mine_keys], preferred_element_type=jnp.float32)
            orows[pl.ds(r, gq, stride=rows_dev), :] = blended + own_weight[part] * new_value[r:r + 1, :]
        att[j, gx] = orows[...].astype(jnp.bfloat16)
        for d in range(1, ZN):
            az_copy(j, d).start()
        ax_copy(j, 0).start()

    def relay(j):
        for d in range(1, ZN):
            az_arrival(j, d).wait_recv()
            ax_copy(j, d).start()

    def output(j):
        for d in range(ZN):
            ax_arrival(j, d).wait_recv()
        for b in range(XN * ZN // 2):
            pair = []
            for s in range(2):
                block = att[j, 2 * b + s].astype(jnp.float32)
                pair.append(jnp.concatenate(
                    [block[h * rows_dev:(h + 1) * rows_dev] for h in range(gq)], axis=1))
            lhs[2 * b * rows_dev:2 * (b + 1) * rows_dev, :] = jnp.concatenate(
                pair, axis=0).astype(jnp.bfloat16)
        wo_copy(j).wait()
        depth = pl.ds(pl.multiple_of(j * group_width, group_width), group_width)

        def one(n, _):
            cols = pl.ds(pl.multiple_of(n * TILE, TILE), TILE)
            acc[:, cols] += jnp.dot(lhs[...], wo[depth, cols], preferred_element_type=jnp.float32)
            return 0
        lax.fori_loop(0, acc.shape[1] // TILE, one, 0)

    def step(t, _):
        for delay, stage in (
                (0, project), (2, across_x), (3, attention), (4, relay), (5, output)):
            if delay == 2:
                pl.when(t == 1)(separate)

            @pl.when((t >= delay) & (t < groups + delay))
            def _(stage=stage, delay=delay):
                stage(t - delay)
        return 0
    lax.fori_loop(0, groups + 5, step, 0)

    psend[...] = acc[theirs, :].astype(jnp.bfloat16)
    last = pltpu.make_async_remote_copy(
        psend, precv, ps_sem, pr_sem, device_id={"gy": ypeer}, device_id_type=MESH)
    last.start()
    last.wait_recv()
    out_ref[...] = (acc[mine, :] + precv[...].astype(jnp.float32)).astype(jnp.bfloat16)
    last.wait_send()

    def drain(j, _):
        for p in range(pieces):
            i = j * pieces + p
            x_copy(i).wait_send()
            for d in range(1, ZN):
                z_copy(i, d).wait_send()
        for d in range(1, ZN):
            az_copy(j, d).wait_send()
        for d in range(ZN):
            ax_copy(j, d).wait_send()
        return 0
    lax.fori_loop(0, groups, drain, 0)


def fused(activations, qkv_weight, out_weight, key_cache, value_cache, lengths):
    rows_dev, context, groups, hd = key_cache.shape
    half_rows, depth = activations.shape
    rows = 2 * half_rows
    qkv_cols = qkv_weight.shape[1]
    heads_in = out_weight.shape[0]
    width = out_weight.shape[1]
    gq = heads_in // (groups * hd)
    block = (gq + 2) * hd
    pieces = 3
    piece = block // pieces
    n = groups * pieces
    bf16, f32 = jnp.bfloat16, jnp.float32

    anywhere = pl.BlockSpec(memory_space=pl.ANY)
    vmem = pl.BlockSpec(memory_space=pltpu.VMEM)
    dma = pltpu.SemaphoreType.DMA
    return pl.pallas_call(
        functools.partial(fused_kernel, (groups, gq, hd, piece, pieces, rows_dev)),
        out_shape=jax.ShapeDtypeStruct((half_rows, width), bf16),
        in_specs=[anywhere] * 5 + [pl.BlockSpec(memory_space=pltpu.SMEM)],
        out_specs=vmem,
        scratch_shapes=[
            pltpu.VMEM((rows, depth), bf16),
            pltpu.VMEM((SLOTS, depth, piece), bf16),
            pltpu.VMEM((heads_in, width), bf16),
            pltpu.VMEM((rows_dev, context * groups, hd), bf16),
            pltpu.VMEM((rows_dev, context * groups, hd), bf16),
            pltpu.VMEM((n, ZN, rows_dev, piece), f32),
            pltpu.VMEM((n, ZN, rows_dev, piece), f32),
            pltpu.VMEM((n, ZN, rows_dev, piece), f32),
            pltpu.VMEM((n, ZN, rows_dev, piece), f32),
            pltpu.VMEM((n, ZN - 1, rows_dev, piece), f32),
            pltpu.VMEM((rows_dev, block), f32),
            pltpu.VMEM((gq * rows_dev, hd), f32),
            pltpu.VMEM((gq * rows_dev, context), f32),
            pltpu.VMEM((gq * rows_dev, hd), f32),
            pltpu.VMEM((context * groups, hd), f32),
            pltpu.VMEM((rows_dev, hd), f32),
            pltpu.VMEM((rows_dev, hd), f32),
            pltpu.VMEM((groups, XN * ZN, gq * rows_dev, hd), bf16),
            pltpu.VMEM((rows, gq * hd), bf16),
            pltpu.VMEM((rows, width), f32),
            pltpu.VMEM((half_rows, width), bf16),
            pltpu.VMEM((half_rows, width), bf16),
            dma((3,)), dma((SLOTS,)), dma((groups,)), dma((2,)),
            dma((n,)), dma((n,)), dma((n, ZN - 1)), dma((n, ZN - 1)),
            dma((groups, ZN - 1)), dma((groups, ZN - 1)), dma((groups, ZN)), dma((groups, ZN)),
            dma, dma,
        ],
        compiler_params=pltpu.CompilerParams(
            collective_id=0, has_side_effects=True, vmem_limit_bytes=63 * 1024 * 1024),
        cost_estimate=pl.CostEstimate(
            flops=2 * rows * (depth * qkv_cols + heads_in * width),
            bytes_accessed=2 * (depth * qkv_cols + heads_in * width), transcendentals=0),
        name="fused_attention",
    )(
        activations, qkv_weight, out_weight,
        key_cache.reshape(rows_dev, context * groups, hd),
        value_cache.reshape(rows_dev, context * groups, hd),
        lengths,
    )


def rotate(vectors, positions):
    half_dim = vectors.shape[-1] // 2
    frequency = 500000.0 ** (-(jnp.arange(half_dim).astype(jnp.float32) * 2.0 / vectors.shape[-1]))
    angles = positions.astype(jnp.float32)[..., None] * frequency
    cosine = jnp.cos(angles)
    sine_part = jnp.sin(angles)
    lower_half = vectors[..., :half_dim]
    upper_half = vectors[..., half_dim:]
    return jnp.concatenate(
        [
            lower_half * cosine - upper_half * sine_part,
            upper_half * cosine + lower_half * sine_part,
        ],
        axis=-1,
    )


def attend(queries, new_key, new_value, keys, values, lengths):
    queries = rotate(queries.astype(jnp.float32), lengths[:, None, None]).astype(jnp.bfloat16)
    new_key = rotate(new_key.astype(jnp.float32), lengths[:, None]).astype(jnp.bfloat16)
    scaling = queries.shape[-1] ** (-0.5)
    scores = (
        jnp.einsum("rgqd,rpgd->rgqp", queries, keys, preferred_element_type=jnp.float32) * scaling
    )
    own_score = (
        jnp.einsum("rgqd,rgd->rgq", queries, new_key, preferred_element_type=jnp.float32) * scaling
    )
    visible = (jnp.arange(keys.shape[1])[None, :] < lengths[:, None])[:, None, None, :]
    masked = jnp.where(visible, scores, -1e30)
    highest = jnp.maximum(jnp.max(masked, axis=-1), own_score)
    raised = jnp.where(visible, jnp.exp(masked - highest[..., None]), 0.0)
    own_raised = jnp.exp(own_score - highest)
    denominator = jnp.sum(raised, axis=-1) + own_raised
    weights = (raised / denominator[..., None]).astype(jnp.bfloat16)
    own_weight = (own_raised / denominator).astype(jnp.bfloat16)
    blended = jnp.einsum("rgqp,rpgd->rgqd", weights, values, preferred_element_type=jnp.float32)
    blended = (
        blended
        + own_weight.astype(jnp.float32)[..., None] * new_value.astype(jnp.float32)[:, :, None, :]
    )
    return blended.astype(jnp.bfloat16)


def local(activations, qkv_weight, out_weight, key_cache, value_cache, lengths):
    rows_dev = key_cache.shape[0]
    head_groups = key_cache.shape[2]
    head_dim = key_cache.shape[3]
    all_rows = lax.all_gather(activations, "gy", axis=0, tiled=True)
    summed = lax.psum_scatter(
        jnp.dot(all_rows, qkv_weight, preferred_element_type=jnp.float32),
        "gx",
        scatter_dimension=0,
        tiled=True,
    )
    projected = summed.astype(jnp.bfloat16).reshape(rows_dev, head_groups, -1, head_dim)
    attended = attend(
        projected[:, :, :-2],
        projected[:, :, -2],
        projected[:, :, -1],
        key_cache,
        value_cache,
        lengths,
    )
    attended = attended.reshape(rows_dev, -1)
    partial_out = jnp.dot(
        lax.all_gather(attended, "gx", axis=0, tiled=True),
        out_weight,
        preferred_element_type=jnp.float32,
    )
    return lax.psum_scatter(partial_out.astype(jnp.bfloat16), "gy", scatter_dimension=0, tiled=True)


def solution(mesh):
    placed = (
        P(("groups", "gy"), "gx"),
        P("gx", "gy"),
        P("gy", "gx"),
        P(("groups", "gx"), None, "gy", None),
        P(("groups", "gx"), None, "gy", None),
        P(("groups", "gx")),
    )
    chosen = fused if mesh.shape["gx"] == XN * ZN and mesh.shape["gy"] == 2 else local
    return jax.shard_map(
        chosen, mesh=mesh, in_specs=placed, out_specs=P(("groups", "gy"), "gx"), check_vma=False
    )
```
